32 devices in a mesh: chain: 4 (over x, core), wide: 8 (over z, y).
Axes of the slice: x: 2, y: 2, z: 4, core: 2. Of those that a mesh axis runs over, the one named last changes fastest.
Arguments:
- right_side: float32 [4, 64, 1024], P('chain', None, 'wide'), may hold values from -6 to 6
- lower_blocks: bfloat16 [4, 4, 64, 64, 1024], P('chain', None, None, None, 'wide'), may hold values from -1 to 1
- lower_index: int32 [4, 4, 1024], P('chain', None, 'wide'), may hold values from 0 to 1023
- upper_blocks: bfloat16 [4, 4, 64, 64, 1024], P('chain', None, None, None, 'wide'), may hold values from -1 to 1
- upper_index: int32 [4, 4, 1024], P('chain', None, 'wide'), may hold values from 0 to 1023
- inverse: bfloat16 [4, 64, 64, 1024], P('chain', None, None, 'wide'), may hold values from -0.5 to 1, as said below
- donor_weight: bfloat16 [4, 64, 64, 1024], P('chain', None, None, 'wide'), may hold values from -1 to 1
- donor_index: int32 [4, 1024], P('chain', 'wide'), may hold values from 0 to 1023
- target: int32 [4, 1024], P('chain', 'wide'), may hold values from 0 to 1023, as said below
Outputs:
- relocated: float32 [4, 64, 1024], P('chain', None, 'wide')
The draws below stay inside these ranges and needn't reach their ends.
Inputs may be any that keep to these rules, and one draw needn't show every extreme that they name: `inverse`: inverses of well-conditioned pivot blocks. For each level set, a permutation of the block rows; block row b of wide index b // 128 goes to wide index target // 128; every wide index receives 128 block rows of a level set and hands at most 32 of them to any one wide index, exactly 32 to some.
All inputs are finite; a program needn't handle non-finite values.
Results may differ from the reference program's by a relative error of at most 0.007.
Values may be sent and summed in bfloat16 or wider, within the bound.
A program may use at most 64 MiB of HBM per device.

```python
import jax
import jax.numpy as jnp

BLOCK = 64
COUPLE = 4
BLOCKS_DEV = 128
HANDOVER_LIMIT = 32
LEVELS = 4
LEVEL_BLOCKS = 1024
N_WIDE = 8


def draw_inverse(key, part):
    base_key = jax.random.fold_in(key, 11)
    rows = jnp.arange(BLOCK)[:, None]
    columns = jnp.arange(BLOCK)[None, :]
    identity = (rows == columns).astype(jnp.float32)[None, :, :, None]
    shape = (LEVELS, BLOCK, BLOCK, LEVEL_BLOCKS)
    noise = jnp.clip(jax.random.normal(base_key, shape, jnp.float32), -6.0, 6.0)
    values = 0.6 * identity + noise * (0.35 / BLOCK ** 0.5)
    return values.astype(jnp.bfloat16)


def level_targets(level_key):
    level_width = N_WIDE
    blocks = BLOCKS_DEV
    random_keys = jax.random.split(level_key, 5)
    remain = blocks - HANDOVER_LIMIT
    level_spread = remain // (level_width - 1)
    excess_rows = remain - level_spread * (level_width - 1)
    extra_rows = (jax.random.permutation(random_keys[0], level_width - 1) < excess_rows).astype(jnp.int32)
    row_loads = jnp.concatenate([jnp.array([HANDOVER_LIMIT], jnp.int32), level_spread + extra_rows])
    sigma = jax.random.permutation(random_keys[1], level_width)
    shifts = jax.random.permutation(random_keys[2], level_width)
    pairs = row_loads[(sigma[None, :] - shifts[:, None]) % level_width]
    running = jnp.cumsum(pairs, axis=1)
    offsets = running - pairs
    places = jnp.arange(blocks)[None, :]
    owners = jnp.sum((places[:, :, None] >= running[:, None, :]).astype(jnp.int32), axis=2)
    within = places - jnp.take_along_axis(offsets, owners, axis=1)
    incoming = jnp.cumsum(pairs, axis=0) - pairs
    arrival = jnp.take_along_axis(incoming, owners, axis=1) + within
    shuffles = jax.vmap(lambda single: jax.random.permutation(single, blocks))(jax.random.split(random_keys[3], level_width))
    slots = shuffles[owners, arrival]
    sorted_targets = owners * blocks + slots
    orders = jax.vmap(lambda single: jax.random.permutation(single, blocks))(jax.random.split(random_keys[4], level_width))
    senders = jnp.arange(level_width)[:, None]
    result = jnp.zeros((level_width, blocks), jnp.int32).at[senders, orders].set(sorted_targets)
    return result.reshape(level_width * blocks)


def draw_target(key, part):
    base_key = jax.random.fold_in(key, 23)
    return jax.vmap(level_targets)(jax.random.split(base_key, LEVELS)).astype(jnp.int32)


def set_ends(values, stream_key, low, top_value):
    extent = values.shape
    index_at = [jax.random.randint(jax.random.fold_in(stream_key, axis), (), 0, extent[axis]) for axis in range(len(extent))]
    values = values.at[tuple(index_at)].set(low)
    longest = extent.index(max(extent))
    index_at[longest] = (index_at[longest] + 1) % extent[longest]
    return values.at[tuple(index_at)].set(top_value)


def levels(key, dims, cuts, least, top_value):
    loudness, own = 1.0, jax.random.fold_in(key, 6)
    for position, parts in cuts:
        steps = jnp.exp(jax.random.uniform(jax.random.fold_in(own, position), (parts,), jnp.float32, least / len(cuts), top_value / len(cuts)))
        loudness = loudness * jnp.repeat(steps, dims[position] // parts).reshape([-1 if axis == position else 1 for axis in range(len(dims))])
    return loudness


def gaussian(stream_key, shape, width, bound, shards=(), held_as=jnp.bfloat16):
    gain = levels(stream_key, shape, shards, -0.22, 0.18) if shards else 1.0
    values = jax.random.normal(stream_key, shape, jnp.float32) * width * gain
    return jnp.minimum(jnp.maximum(values, -bound), bound).astype(held_as)


def setup_inputs(seed: int = 0) -> dict:
    splits = jax.random.split(jax.random.key(seed), 10)
    return {
        "right_side": gaussian(splits[0], (LEVELS, BLOCK, LEVEL_BLOCKS), 1.0, 6.0, ((0, 4), (2, 8)), jnp.float32),
        "lower_blocks": gaussian(splits[1], (LEVELS, COUPLE, BLOCK, BLOCK, LEVEL_BLOCKS), (1.1 / (BLOCK * COUPLE) ** 0.5), 1.0, ((0, 4), (4, 8))),
        "lower_index": set_ends(jax.random.randint(splits[2], (LEVELS, COUPLE, LEVEL_BLOCKS), 0, LEVEL_BLOCKS), jax.random.fold_in(splits[2], 1), 0, LEVEL_BLOCKS - 1).astype(jnp.int32),
        "upper_blocks": gaussian(splits[3], (LEVELS, COUPLE, BLOCK, BLOCK, LEVEL_BLOCKS), (1.1 / (BLOCK * COUPLE) ** 0.5), 1.0, ((0, 4), (4, 8))),
        "upper_index": set_ends(jax.random.randint(splits[4], (LEVELS, COUPLE, LEVEL_BLOCKS), 0, LEVEL_BLOCKS), jax.random.fold_in(splits[4], 1), 0, LEVEL_BLOCKS - 1).astype(jnp.int32),
        "inverse": draw_inverse(jax.random.fold_in(splits[9], 71), 0),
        "donor_weight": gaussian(splits[6], (LEVELS, BLOCK, BLOCK, LEVEL_BLOCKS), (0.6 / BLOCK ** 0.5), 1.0, ((0, 4), (3, 8))),
        "donor_index": set_ends(jax.random.randint(splits[7], (LEVELS, LEVEL_BLOCKS), 0, LEVEL_BLOCKS), jax.random.fold_in(splits[7], 1), 0, LEVEL_BLOCKS - 1).astype(jnp.int32),
        "target": draw_target(jax.random.fold_in(splits[9], 71), 0),
    }


def couple(blocks, index, vector):
    picked = jnp.take(vector, index, axis=1).astype(jnp.float32)
    return jnp.einsum("kijb,jkb->ib", blocks.astype(jnp.float32), picked)


def apply_inverse(inverse_level, values):
    rounded = values.astype(jnp.bfloat16).astype(jnp.float32)
    return jnp.einsum("ijb,jb->ib", inverse_level.astype(jnp.float32), rounded)


def reference(right_side, lower_blocks, lower_index, upper_blocks, upper_index, inverse, donor_weight, donor_index, target):
    forward = []
    previous = None
    for level in range(LEVELS):
        rounded = right_side[level].astype(jnp.bfloat16)
        picked = jnp.take(rounded, donor_index[level], axis=1).astype(jnp.float32)
        source = right_side[level] + jnp.einsum("ijb,jb->ib", donor_weight[level].astype(jnp.float32), picked)
        if level > 0:
            source = source - couple(lower_blocks[level], lower_index[level], previous.astype(jnp.bfloat16))
        current = apply_inverse(inverse[level], source)
        forward.append(current)
        previous = current
    backward = [None] * LEVELS
    following = None
    for level in reversed(range(LEVELS)):
        if level == LEVELS - 1:
            current = forward[level]
        else:
            current = forward[level] - apply_inverse(inverse[level], couple(upper_blocks[level], upper_index[level], following.astype(jnp.bfloat16)))
        backward[level] = current
        following = current
    placed = []
    for level in range(LEVELS):
        empty = jnp.zeros((BLOCK, LEVEL_BLOCKS), jnp.float32)
        placed.append(empty.at[:, target[level]].set(backward[level]))
    return jnp.stack(placed)
```

```python
import functools

import jax
import jax.numpy as jnp
from jax import lax
from jax.experimental import pallas as pl
from jax.experimental.pallas import tpu as pltpu
from jax.sharding import PartitionSpec as P

MESH = pl.DeviceIdType.MESH
LANES = 128


def apply_blocks(blocks, vector, result):
    couples, rows, unknowns, width = blocks.shape
    group = 8

    def body(step, _):
        first = pl.multiple_of(step * group, group)
        total = jnp.zeros((group, 16, width), jnp.float32)
        for k in range(couples):
            for j in range(0, unknowns, 16):
                block = blocks[k, pl.ds(first, group), j : j + 16, :].astype(jnp.float32)
                total += block * vector[k, j : j + 16, :][None]
        result[pl.ds(first, group), :] = jnp.sum(total, axis=1)
        return 0

    lax.fori_loop(0, rows // group, body, 0)


def kernel(
    chain_count,
    wide_count,
    rhs,
    lower_hbm,
    lower_index,
    upper_hbm,
    upper_index,
    inverse_hbm,
    donor_hbm,
    donor_index,
    target,
    out,
    lower,
    upper,
    inverse,
    donor,
    rhs_all,
    forward_all,
    backward_all,
    final_all,
    target_all,
    rhs_send,
    forward_send,
    solved_send,
    picked,
    vector,
    product,
    source,
    forward,
    places,
    load_sem,
    send_sem,
    recv_sem,
):
    level = lax.axis_index("chain")
    me = lax.axis_index("wide")
    unknowns, width = source.shape

    loads = [
        pltpu.make_async_copy(hbm.at[0], vmem, load_sem.at[number])
        for number, (hbm, vmem) in enumerate(
            ((donor_hbm, donor.at[0]), (inverse_hbm, inverse.at[0]), (lower_hbm, lower), (upper_hbm, upper))
        )
    ]
    for load in loads:
        load.start()

    barrier = pltpu.get_barrier_semaphore()
    for step in range(1, wide_count):
        pl.semaphore_signal(
            barrier, inc=1, device_id=(level, lax.rem(me + step, wide_count)), device_id_type=MESH
        )

    @pl.when(level > 0)
    def _():
        for other in range(wide_count):
            pl.semaphore_signal(barrier, inc=1, device_id=(level - 1, other), device_id_type=MESH)

    @pl.when(level < chain_count - 1)
    def _():
        for other in range(wide_count):
            pl.semaphore_signal(barrier, inc=1, device_id=(level + 1, other), device_id_type=MESH)

    rhs_send[...] = rhs[0].astype(jnp.bfloat16)
    rhs_all[me] = rhs_send[...]
    target_all[me] = target[...]

    at_end = (level == 0) | (level == chain_count - 1)

    @pl.when(at_end)
    def _():
        pl.semaphore_wait(barrier, 2 * wide_count - 1)

    @pl.when(jnp.logical_not(at_end))
    def _():
        pl.semaphore_wait(barrier, 3 * wide_count - 1)

    def copy_to(value, gathered, phase, chain, other):
        return pltpu.make_async_remote_copy(
            src_ref=value,
            dst_ref=gathered.at[me],
            send_sem=send_sem.at[phase, other],
            recv_sem=recv_sem.at[phase, me],
            device_id=(chain, other),
            device_id_type=MESH,
        )

    def peers():
        return [lax.rem(me + step, wide_count) for step in range(1, wide_count)]

    def arrival(value, gathered, phase, other):
        return pltpu.make_async_remote_copy(
            src_ref=value,
            dst_ref=gathered.at[other],
            send_sem=send_sem.at[phase, other],
            recv_sem=recv_sem.at[phase, other],
            device_id=(level, other),
            device_id_type=MESH,
        )

    def send_across(value, gathered, phase):
        for other in peers():
            copy_to(value, gathered, phase, level, other).start()

    def sent_across(value, gathered, phase):
        for other in peers():
            copy_to(value, gathered, phase, level, other).wait_send()

    def arrive_across(value, gathered, phase):
        for other in peers():
            arrival(value, gathered, phase, other).wait_recv()

    def send_along(value, gathered, phase, chain):
        for step in range(wide_count):
            copy_to(value, gathered, phase, chain, lax.rem(me + step, wide_count)).start()

    def sent_along(value, gathered, phase, chain):
        for step in range(wide_count):
            copy_to(value, gathered, phase, chain, lax.rem(me + step, wide_count)).wait_send()

    def pick(gathered, index, arrive):
        couples = index.shape[0]
        lanes = [jnp.broadcast_to(index[k : k + 1] % LANES, (unknowns, width)) for k in range(couples)]
        tiles = [jnp.broadcast_to(index[k : k + 1] // LANES, (unknowns, width)) for k in range(couples)]
        for other in range(wide_count):
            arrive(other)
            tile = gathered[other].astype(jnp.float32)
            for k in range(couples):
                found = jnp.take_along_axis(tile, lanes[k], axis=1, mode="promise_in_bounds")
                if other == 0:
                    picked[k] = found
                else:
                    picked[k] = jnp.where(tiles[k] == other, found, picked[k])

    send_across(rhs_send, rhs_all, 0)
    send_across(target, target_all, 1)
    arrive_across(rhs_send, rhs_all, 0)
    pick(rhs_all, donor_index[...], lambda other: None)
    loads[0].wait()
    apply_blocks(donor, picked.at[0:1], product)
    source[...] = rhs[0] + product[...]
    loads[1].wait()
    loads[2].wait()

    @pl.when(level > 0)
    def _():
        pick(
            forward_all,
            lower_index[0],
            lambda other: arrival(forward_send, forward_all, 2, other).wait_recv(),
        )
        apply_blocks(lower, picked, product)
        source[...] -= product[...]

    vector[0] = source[...].astype(jnp.bfloat16).astype(jnp.float32)
    apply_blocks(inverse, vector, forward)
    loads[3].wait()

    @pl.when(level < chain_count - 1)
    def _():
        forward_send[...] = forward[...].astype(jnp.bfloat16)
        send_along(forward_send, forward_all, 2, level + 1)

    arrive_across(target, target_all, 1)
    spots = me * width + lax.broadcasted_iota(jnp.int32, (width, width), 0)
    for other in range(wide_count):
        hit = spots == jnp.broadcast_to(target_all[other], (width, width))
        places[:, other * width : (other + 1) * width] = jnp.where(hit, 1.0, 0.0).astype(jnp.bfloat16)

    @pl.when(level < chain_count - 1)
    def _():
        pick(
            backward_all,
            upper_index[0],
            lambda other: arrival(solved_send, backward_all, 3, other).wait_recv(),
        )
        apply_blocks(upper, picked, product)
        vector[0] = product[...].astype(jnp.bfloat16).astype(jnp.float32)
        apply_blocks(inverse, vector, product)
        forward[...] -= product[...]

    solved_send[...] = forward[...].astype(jnp.bfloat16)

    @pl.when(level > 0)
    def _():
        send_along(solved_send, backward_all, 3, level - 1)

    final_all[me] = solved_send[...]
    send_across(solved_send, final_all, 4)
    arrive_across(solved_send, final_all, 4)
    placed = jnp.zeros((unknowns, width), jnp.float32)
    for other in range(wide_count):
        placed += lax.dot_general(
            final_all[other],
            places[:, other * width : (other + 1) * width],
            (((1,), (1,)), ((), ())),
            preferred_element_type=jnp.float32,
        )
    out[0] = placed

    sent_across(rhs_send, rhs_all, 0)
    sent_across(target, target_all, 1)

    @pl.when(level < chain_count - 1)
    def _():
        sent_along(forward_send, forward_all, 2, level + 1)

    @pl.when(level > 0)
    def _():
        sent_along(solved_send, backward_all, 3, level - 1)

    sent_across(solved_send, final_all, 4)


def solution(mesh):
    in_specs = (
        P("chain", None, "wide"),
        P("chain", None, None, None, "wide"),
        P("chain", None, "wide"),
        P("chain", None, None, None, "wide"),
        P("chain", None, "wide"),
        P("chain", None, None, "wide"),
        P("chain", None, None, "wide"),
        P("chain", "wide"),
        P("chain", "wide"),
    )
    out_specs = P("chain", None, "wide")
    chain_count, wide_count = mesh.shape["chain"], mesh.shape["wide"]

    def per_device(rhs, lower, lower_index, upper, upper_index, inverse, donor, donor_index, target):
        _, couples, unknowns, _, width = lower.shape
        inside = pl.BlockSpec(memory_space=pltpu.VMEM)
        outside = pl.BlockSpec(memory_space=pl.ANY)
        tile16 = pltpu.VMEM((unknowns, width), jnp.bfloat16)
        tile32 = pltpu.VMEM((unknowns, width), jnp.float32)
        gathered = pltpu.VMEM((wide_count, unknowns, width), jnp.bfloat16)
        return pl.pallas_call(
            functools.partial(kernel, chain_count, wide_count),
            out_shape=jax.ShapeDtypeStruct(rhs.shape, jnp.float32),
            in_specs=[inside, outside, inside, outside, inside, outside, outside, inside, inside],
            out_specs=inside,
            scratch_shapes=[
                pltpu.VMEM((couples, unknowns, unknowns, width), jnp.bfloat16),
                pltpu.VMEM((couples, unknowns, unknowns, width), jnp.bfloat16),
                pltpu.VMEM((1, unknowns, unknowns, width), jnp.bfloat16),
                pltpu.VMEM((1, unknowns, unknowns, width), jnp.bfloat16),
                gathered,
                gathered,
                gathered,
                gathered,
                pltpu.VMEM((wide_count, 1, width), jnp.int32),
                tile16,
                tile16,
                tile16,
                pltpu.VMEM((couples, unknowns, width), jnp.float32),
                pltpu.VMEM((1, unknowns, width), jnp.float32),
                tile32,
                tile32,
                tile32,
                pltpu.VMEM((width, wide_count * width), jnp.bfloat16),
                pltpu.SemaphoreType.DMA((4,)),
                pltpu.SemaphoreType.DMA((5, wide_count)),
                pltpu.SemaphoreType.DMA((5, wide_count)),
            ],
            compiler_params=pltpu.CompilerParams(
                collective_id=0, has_side_effects=True, vmem_limit_bytes=63 * 1024 * 1024
            ),
        )(rhs, lower, lower_index, upper, upper_index, inverse, donor, donor_index, target)

    return jax.shard_map(
        per_device, mesh=mesh, in_specs=in_specs, out_specs=out_specs, check_vma=False
    )
```

```python
import functools

import jax
import jax.numpy as jnp
from jax import lax
from jax.experimental import pallas as pl
from jax.experimental.pallas import tpu as pltpu
from jax.sharding import PartitionSpec as P

MESH = pl.DeviceIdType.MESH


def apply_blocks(blocks, vector, result):
    couples, rows, unknowns, width = blocks.shape
    group = 8

    def body(step, _):
        first = pl.multiple_of(step * group, group)
        total = jnp.zeros((group, 16, width), jnp.float32)
        for k in range(couples):
            for j in range(0, unknowns, 16):
                block = blocks[k, pl.ds(first, group), j : j + 16, :].astype(jnp.float32)
                total += block * vector[k, j : j + 16, :][None]
        result[pl.ds(first, group), :] = jnp.sum(total, axis=1)
        return 0

    lax.fori_loop(0, rows // group, body, 0)


def kernel(
    chain_count,
    wide_count,
    rhs_hbm,
    lower_hbm,
    lower_index_hbm,
    upper_hbm,
    upper_index_hbm,
    inverse_hbm,
    donor_hbm,
    donor_index_hbm,
    target_hbm,
    out,
    rhs,
    lower_index,
    upper_index,
    donor_index,
    target,
    lower,
    upper,
    inverse,
    donor,
    rhs_all,
    forward_all,
    backward_all,
    final_all,
    target_all,
    rhs_send,
    forward_send,
    solved_send,
    picked,
    vector,
    product,
    source,
    forward,
    places,
    donor_chosen,
    lower_chosen,
    upper_chosen,
    load_sem,
    send_sem,
    recv_sem,
):
    level = lax.axis_index("chain")
    me = lax.axis_index("wide")
    unknowns, width = source.shape

    def partner(step):
        other, digit = 0, 1
        while digit < wide_count:
            mine = lax.rem(me // digit, 2)
            other = other + digit * (1 - mine if step & digit else mine)
            digit *= 2
        return other

    everyone = [partner(step) for step in range(wide_count)]
    peers = everyone[1:]

    barrier = pltpu.get_barrier_semaphore()

    @pl.when(level > 0)
    def _():
        for other in reversed(everyone):
            pl.semaphore_signal(barrier, inc=1, device_id=(level - 1, other), device_id_type=MESH)

    @pl.when(level < chain_count - 1)
    def _():
        for other in reversed(everyone):
            pl.semaphore_signal(barrier, inc=1, device_id=(level + 1, other), device_id_type=MESH)

    for other in reversed(peers):
        pl.semaphore_signal(barrier, inc=1, device_id=(level, other), device_id_type=MESH)

    loads = [
        pltpu.make_async_copy(outer, inner, load_sem.at[number])
        for number, (outer, inner) in enumerate(
            (
                (rhs_hbm.at[0], rhs),
                (target_hbm, target),
                (donor_index_hbm, donor_index),
                (donor_hbm.at[0], donor.at[0]),
                (lower_index_hbm.at[0], lower_index),
                (upper_index_hbm.at[0], upper_index),
                (inverse_hbm.at[0], inverse.at[0]),
                (lower_hbm.at[0], lower),
                (upper_hbm.at[0], upper),
            )
        )
    ]
    for load in loads:
        load.start()

    loads[0].wait()
    loads[1].wait()
    rhs_send[...] = rhs[...].astype(jnp.bfloat16)
    rhs_all[me] = rhs_send[...]
    target_all[me] = target[...]

    at_end = (level == 0) | (level == chain_count - 1)

    @pl.when(at_end)
    def _():
        pl.semaphore_wait(barrier, 2 * wide_count - 1)

    @pl.when(jnp.logical_not(at_end))
    def _():
        pl.semaphore_wait(barrier, 3 * wide_count - 1)

    def copy_to(value, gathered, phase, chain, other):
        return pltpu.make_async_remote_copy(
            src_ref=value,
            dst_ref=gathered.at[me],
            send_sem=send_sem.at[phase, other],
            recv_sem=recv_sem.at[phase, me],
            device_id=(chain, other),
            device_id_type=MESH,
        )

    def arrival(value, gathered, phase, other):
        return pltpu.make_async_remote_copy(
            src_ref=value,
            dst_ref=gathered.at[other],
            send_sem=send_sem.at[phase, other],
            recv_sem=recv_sem.at[phase, other],
            device_id=(level, other),
            device_id_type=MESH,
        )

    def send_across(value, gathered, phase):
        for other in reversed(peers):
            copy_to(value, gathered, phase, level, other).start()

    def sent_across(value, gathered, phase):
        for other in peers:
            copy_to(value, gathered, phase, level, other).wait_send()

    def arrive_across(value, gathered, phase):
        for other in peers:
            arrival(value, gathered, phase, other).wait_recv()

    def send_along(value, gathered, phase, chain):
        for other in reversed(everyone):
            copy_to(value, gathered, phase, chain, other).start()

    def sent_along(value, gathered, phase, chain):
        for other in everyone:
            copy_to(value, gathered, phase, chain, other).wait_send()

    def choose(index, chosen):
        for k in range(index.shape[0]):
            wanted = jnp.broadcast_to(index[k : k + 1], (width, width))
            for other in range(wide_count):
                columns = other * width + lax.broadcasted_iota(jnp.int32, (width, width), 0)
                chosen[other, :, k * width : (k + 1) * width] = jnp.where(
                    columns == wanted, 1.0, 0.0
                ).astype(jnp.bfloat16)

    def pick(gathered, chosen, arrive):
        couples = chosen.shape[2] // width
        total = jnp.zeros((unknowns, couples * width), jnp.float32)
        for step, other in enumerate(everyone):
            arrive(step, other)
            total += jnp.dot(gathered[other], chosen[other], preferred_element_type=jnp.float32)
        for k in range(couples):
            picked[k] = total[:, k * width : (k + 1) * width]

    send_across(rhs_send, rhs_all, 0)
    send_across(target, target_all, 1)
    loads[2].wait()

    def arrive_rhs(step, other):
        if step > 0:
            arrival(rhs_send, rhs_all, 0, other).wait_recv()

    choose(donor_index[...], donor_chosen)
    pick(rhs_all, donor_chosen, arrive_rhs)
    loads[3].wait()
    apply_blocks(donor, picked.at[0:1], product)
    source[...] = rhs[...] + product[...]
    for load in loads[4:8]:
        load.wait()

    @pl.when(level > 0)
    def _():
        choose(lower_index[...], lower_chosen)
        pick(
            forward_all,
            lower_chosen,
            lambda step, other: arrival(forward_send, forward_all, 2, other).wait_recv(),
        )
        apply_blocks(lower, picked, product)
        source[...] -= product[...]

    vector[0] = source[...].astype(jnp.bfloat16).astype(jnp.float32)
    apply_blocks(inverse, vector, forward)
    loads[8].wait()

    @pl.when(level < chain_count - 1)
    def _():
        forward_send[...] = forward[...].astype(jnp.bfloat16)
        send_along(forward_send, forward_all, 2, level + 1)

    arrive_across(target, target_all, 1)
    spots = me * width + lax.broadcasted_iota(jnp.int32, (width, width), 0)
    for other in range(wide_count):
        hit = spots == jnp.broadcast_to(target_all[other], (width, width))
        places[other] = jnp.where(hit, 1.0, 0.0).astype(jnp.bfloat16)

    @pl.when(level < chain_count - 1)
    def _():
        choose(upper_index[...], upper_chosen)
        pick(
            backward_all,
            upper_chosen,
            lambda step, other: arrival(solved_send, backward_all, 3, other).wait_recv(),
        )
        apply_blocks(upper, picked, product)
        vector[0] = product[...].astype(jnp.bfloat16).astype(jnp.float32)
        apply_blocks(inverse, vector, product)
        forward[...] -= product[...]

    solved_send[...] = forward[...].astype(jnp.bfloat16)

    @pl.when(level > 0)
    def _():
        send_along(solved_send, backward_all, 3, level - 1)

    final_all[me] = solved_send[...]
    send_across(solved_send, final_all, 4)
    placed = jnp.zeros((unknowns, width), jnp.float32)
    for step, other in enumerate(everyone):
        if step > 0:
            arrival(solved_send, final_all, 4, other).wait_recv()
        placed += lax.dot_general(
            final_all[other],
            places[other],
            (((1,), (1,)), ((), ())),
            preferred_element_type=jnp.float32,
        )
    out[0] = placed

    sent_across(rhs_send, rhs_all, 0)
    sent_across(target, target_all, 1)

    @pl.when(level < chain_count - 1)
    def _():
        sent_along(forward_send, forward_all, 2, level + 1)

    @pl.when(level > 0)
    def _():
        sent_along(solved_send, backward_all, 3, level - 1)

    sent_across(solved_send, final_all, 4)


def solution(mesh):
    in_specs = (
        P("chain", None, "wide"),
        P("chain", None, None, None, "wide"),
        P("chain", None, "wide"),
        P("chain", None, None, None, "wide"),
        P("chain", None, "wide"),
        P("chain", None, None, "wide"),
        P("chain", None, None, "wide"),
        P("chain", "wide"),
        P("chain", "wide"),
    )
    out_specs = P("chain", None, "wide")
    chain_count, wide_count = mesh.shape["chain"], mesh.shape["wide"]

    def per_device(rhs, lower, lower_index, upper, upper_index, inverse, donor, donor_index, target):
        _, couples, unknowns, _, width = lower.shape
        inside = pl.BlockSpec(memory_space=pltpu.VMEM)
        outside = pl.BlockSpec(memory_space=pl.ANY)
        tile16 = pltpu.VMEM((unknowns, width), jnp.bfloat16)
        tile32 = pltpu.VMEM((unknowns, width), jnp.float32)
        gathered = pltpu.VMEM((wide_count, unknowns, width), jnp.bfloat16)
        return pl.pallas_call(
            functools.partial(kernel, chain_count, wide_count),
            out_shape=jax.ShapeDtypeStruct(rhs.shape, jnp.float32),
            in_specs=[outside] * 9,
            out_specs=inside,
            scratch_shapes=[
                tile32,
                pltpu.VMEM((couples, width), jnp.int32),
                pltpu.VMEM((couples, width), jnp.int32),
                pltpu.VMEM((1, width), jnp.int32),
                pltpu.VMEM((1, width), jnp.int32),
                pltpu.VMEM((couples, unknowns, unknowns, width), jnp.bfloat16),
                pltpu.VMEM((couples, unknowns, unknowns, width), jnp.bfloat16),
                pltpu.VMEM((1, unknowns, unknowns, width), jnp.bfloat16),
                pltpu.VMEM((1, unknowns, unknowns, width), jnp.bfloat16),
                gathered,
                gathered,
                gathered,
                gathered,
                pltpu.VMEM((wide_count, 1, width), jnp.int32),
                tile16,
                tile16,
                tile16,
                pltpu.VMEM((couples, unknowns, width), jnp.float32),
                pltpu.VMEM((1, unknowns, width), jnp.float32),
                tile32,
                tile32,
                tile32,
                pltpu.VMEM((wide_count, width, width), jnp.bfloat16),
                pltpu.VMEM((wide_count, width, width), jnp.bfloat16),
                pltpu.VMEM((wide_count, width, couples * width), jnp.bfloat16),
                pltpu.VMEM((wide_count, width, couples * width), jnp.bfloat16),
                pltpu.SemaphoreType.DMA((9,)),
                pltpu.SemaphoreType.DMA((5, wide_count)),
                pltpu.SemaphoreType.DMA((5, wide_count)),
            ],
            compiler_params=pltpu.CompilerParams(
                collective_id=0, has_side_effects=True, vmem_limit_bytes=63 * 1024 * 1024
            ),
        )(rhs, lower, lower_index, upper, upper_index, inverse, donor, donor_index, target)

    return jax.shard_map(
        per_device, mesh=mesh, in_specs=in_specs, out_specs=out_specs, check_vma=False
    )
```

```python
import functools

import jax
import jax.numpy as jnp
from jax import lax
from jax.experimental import pallas as pl
from jax.experimental.pallas import tpu as pltpu
from jax.sharding import PartitionSpec as P

MESH = pl.DeviceIdType.MESH


def apply_blocks(blocks, vector, result, part=0, parts=1):
    couples, rows, unknowns, width = blocks.shape
    group = 8

    def body(step, _):
        first = pl.multiple_of(step * group, group)
        total = jnp.zeros((group, 16, width), jnp.float32)
        for k in range(couples):
            for j in range(0, unknowns, 16):
                block = blocks[k, pl.ds(first, group), j : j + 16, :].astype(jnp.float32)
                total += block * vector[k, j : j + 16, :][None]
        result[pl.ds(first, group), :] = jnp.sum(total, axis=1)
        return 0

    steps = rows // group // parts
    lax.fori_loop(part * steps, (part + 1) * steps, body, 0)


def kernel(
    chain_count,
    wide_count,
    rhs_hbm,
    lower_hbm,
    lower_index_hbm,
    upper_hbm,
    upper_index_hbm,
    inverse_hbm,
    donor_hbm,
    donor_index_hbm,
    target_hbm,
    out,
    rhs,
    lower_index,
    upper_index,
    donor_index,
    target,
    lower,
    upper,
    inverse,
    donor,
    rhs_all,
    forward_all,
    backward_all,
    final_all,
    target_all,
    rhs_send,
    forward_send,
    solved_send,
    picked,
    vector,
    product,
    source,
    forward,
    places,
    donor_chosen,
    lower_chosen,
    upper_chosen,
    load_sem,
    send_sem,
    recv_sem,
):
    level = lax.axis_index("chain")
    me = lax.axis_index("wide")
    unknowns, width = source.shape

    def partner(step):
        other, digit = 0, 1
        while digit < wide_count:
            mine = lax.rem(me // digit, 2)
            other = other + digit * (1 - mine if step & digit else mine)
            digit *= 2
        return other

    everyone = [partner(step) for step in range(wide_count)]
    peers = everyone[1:]

    barrier = pltpu.get_barrier_semaphore()

    @pl.when(level > 0)
    def _():
        for other in reversed(everyone):
            pl.semaphore_signal(barrier, inc=1, device_id=(level - 1, other), device_id_type=MESH)

    @pl.when(level < chain_count - 1)
    def _():
        for other in reversed(everyone):
            pl.semaphore_signal(barrier, inc=1, device_id=(level + 1, other), device_id_type=MESH)

    for other in reversed(peers):
        pl.semaphore_signal(barrier, inc=1, device_id=(level, other), device_id_type=MESH)

    loads = [
        pltpu.make_async_copy(outer, inner, load_sem.at[number])
        for number, (outer, inner) in enumerate(
            (
                (rhs_hbm.at[0], rhs),
                (target_hbm, target),
                (donor_index_hbm, donor_index),
                (donor_hbm.at[0], donor.at[0]),
                (lower_index_hbm.at[0], lower_index),
                (upper_index_hbm.at[0], upper_index),
                (inverse_hbm.at[0], inverse.at[0]),
                (lower_hbm.at[0], lower),
                (upper_hbm.at[0], upper),
            )
        )
    ]
    for load in loads:
        load.start()

    loads[0].wait()
    loads[1].wait()
    rhs_send[...] = rhs[...].astype(jnp.bfloat16)
    rhs_all[me] = rhs_send[...]
    target_all[me] = target[...]

    at_end = (level == 0) | (level == chain_count - 1)

    @pl.when(at_end)
    def _():
        pl.semaphore_wait(barrier, 2 * wide_count - 1)

    @pl.when(jnp.logical_not(at_end))
    def _():
        pl.semaphore_wait(barrier, 3 * wide_count - 1)

    def copy_to(value, gathered, phase, chain, other):
        return pltpu.make_async_remote_copy(
            src_ref=value,
            dst_ref=gathered.at[me],
            send_sem=send_sem.at[phase, other],
            recv_sem=recv_sem.at[phase, me],
            device_id=(chain, other),
            device_id_type=MESH,
        )

    def arrival(value, gathered, phase, other):
        return pltpu.make_async_remote_copy(
            src_ref=value,
            dst_ref=gathered.at[other],
            send_sem=send_sem.at[phase, other],
            recv_sem=recv_sem.at[phase, other],
            device_id=(level, other),
            device_id_type=MESH,
        )

    def send_across(value, gathered, phase):
        for other in reversed(peers):
            copy_to(value, gathered, phase, level, other).start()

    def sent_across(value, gathered, phase):
        for other in peers:
            copy_to(value, gathered, phase, level, other).wait_send()

    def arrive_across(value, gathered, phase):
        for other in peers:
            arrival(value, gathered, phase, other).wait_recv()

    def half_to(value, gathered, phase, chain, other, half):
        rows = pl.ds(half * (unknowns // 2), unknowns // 2)
        return pltpu.make_async_remote_copy(
            src_ref=value.at[rows],
            dst_ref=gathered.at[me, rows],
            send_sem=send_sem.at[phase + half, other],
            recv_sem=recv_sem.at[phase + half, me],
            device_id=(chain, other),
            device_id_type=MESH,
        )

    def half_from(value, gathered, phase, other, half):
        rows = pl.ds(half * (unknowns // 2), unknowns // 2)
        return pltpu.make_async_remote_copy(
            src_ref=value.at[rows],
            dst_ref=gathered.at[other, rows],
            send_sem=send_sem.at[phase + half, other],
            recv_sem=recv_sem.at[phase + half, other],
            device_id=(level, other),
            device_id_type=MESH,
        )

    def send_along(value, gathered, phase, chain, half):
        for other in reversed(everyone):
            half_to(value, gathered, phase, chain, other, half).start()

    def sent_along(value, gathered, phase, chain):
        for half in range(2):
            for other in everyone:
                half_to(value, gathered, phase, chain, other, half).wait_send()

    def arrive_along(value, gathered, phase, other):
        for half in range(2):
            half_from(value, gathered, phase, other, half).wait_recv()

    def choose(index, chosen):
        for k in range(index.shape[0]):
            wanted = jnp.broadcast_to(index[k : k + 1], (width, width))
            for other in range(wide_count):
                columns = other * width + lax.broadcasted_iota(jnp.int32, (width, width), 0)
                chosen[other, :, k * width : (k + 1) * width] = jnp.where(
                    columns == wanted, 1.0, 0.0
                ).astype(jnp.bfloat16)

    def pick(gathered, chosen, arrive):
        couples = chosen.shape[2] // width
        total = jnp.zeros((unknowns, couples * width), jnp.float32)
        for step, other in enumerate(everyone):
            arrive(step, other)
            total += jnp.dot(gathered[other], chosen[other], preferred_element_type=jnp.float32)
        for k in range(couples):
            picked[k] = total[:, k * width : (k + 1) * width]

    def find_places():
        arrive_across(target, target_all, 1)
        spots = me * width + lax.broadcasted_iota(jnp.int32, (width, width), 0)
        for other in range(wide_count):
            hit = spots == jnp.broadcast_to(target_all[other], (width, width))
            places[other] = jnp.where(hit, 1.0, 0.0).astype(jnp.bfloat16)

    send_across(rhs_send, rhs_all, 0)
    send_across(target, target_all, 1)
    loads[2].wait()

    def arrive_rhs(step, other):
        if step > 0:
            arrival(rhs_send, rhs_all, 0, other).wait_recv()

    choose(donor_index[...], donor_chosen)
    pick(rhs_all, donor_chosen, arrive_rhs)
    loads[3].wait()
    apply_blocks(donor, picked.at[0:1], product)
    source[...] = rhs[...] + product[...]
    for load in loads[4:8]:
        load.wait()

    @pl.when(level > 0)
    def _():
        choose(lower_index[...], lower_chosen)
        find_places()
        pick(
            forward_all,
            lower_chosen,
            lambda step, other: arrive_along(forward_send, forward_all, 2, other),
        )
        apply_blocks(lower, picked, product)
        source[...] -= product[...]

    vector[0] = source[...].astype(jnp.bfloat16).astype(jnp.float32)
    for half in range(2):
        apply_blocks(inverse, vector, forward, half, 2)
        rows = slice(half * (unknowns // 2), (half + 1) * (unknowns // 2))
        forward_send[rows] = forward[rows].astype(jnp.bfloat16)

        @pl.when(level < chain_count - 1)
        def _():
            send_along(forward_send, forward_all, 2, level + 1, half)

    loads[8].wait()

    @pl.when(level == 0)
    def _():
        find_places()

    @pl.when(level < chain_count - 1)
    def _():
        choose(upper_index[...], upper_chosen)
        pick(
            backward_all,
            upper_chosen,
            lambda step, other: arrive_along(solved_send, backward_all, 4, other),
        )
        apply_blocks(upper, picked, product)
        vector[0] = product[...].astype(jnp.bfloat16).astype(jnp.float32)

    for half in range(2):
        rows = slice(half * (unknowns // 2), (half + 1) * (unknowns // 2))

        @pl.when(level < chain_count - 1)
        def _():
            apply_blocks(inverse, vector, product, half, 2)
            forward[rows] -= product[rows]

        solved_send[rows] = forward[rows].astype(jnp.bfloat16)

        @pl.when(level > 0)
        def _():
            send_along(solved_send, backward_all, 4, level - 1, half)

    final_all[me] = solved_send[...]
    send_across(solved_send, final_all, 6)
    placed = jnp.zeros((unknowns, width), jnp.float32)
    for step, other in enumerate(everyone):
        if step > 0:
            arrival(solved_send, final_all, 6, other).wait_recv()
        placed += lax.dot_general(
            final_all[other],
            places[other],
            (((1,), (1,)), ((), ())),
            preferred_element_type=jnp.float32,
        )
    out[0] = placed

    sent_across(rhs_send, rhs_all, 0)
    sent_across(target, target_all, 1)

    @pl.when(level < chain_count - 1)
    def _():
        sent_along(forward_send, forward_all, 2, level + 1)

    @pl.when(level > 0)
    def _():
        sent_along(solved_send, backward_all, 4, level - 1)

    sent_across(solved_send, final_all, 6)


def solution(mesh):
    in_specs = (
        P("chain", None, "wide"),
        P("chain", None, None, None, "wide"),
        P("chain", None, "wide"),
        P("chain", None, None, None, "wide"),
        P("chain", None, "wide"),
        P("chain", None, None, "wide"),
        P("chain", None, None, "wide"),
        P("chain", "wide"),
        P("chain", "wide"),
    )
    out_specs = P("chain", None, "wide")
    chain_count, wide_count = mesh.shape["chain"], mesh.shape["wide"]

    def per_device(rhs, lower, lower_index, upper, upper_index, inverse, donor, donor_index, target):
        _, couples, unknowns, _, width = lower.shape
        inside = pl.BlockSpec(memory_space=pltpu.VMEM)
        outside = pl.BlockSpec(memory_space=pl.ANY)
        tile16 = pltpu.VMEM((unknowns, width), jnp.bfloat16)
        tile32 = pltpu.VMEM((unknowns, width), jnp.float32)
        gathered = pltpu.VMEM((wide_count, unknowns, width), jnp.bfloat16)
        return pl.pallas_call(
            functools.partial(kernel, chain_count, wide_count),
            out_shape=jax.ShapeDtypeStruct(rhs.shape, jnp.float32),
            in_specs=[outside] * 9,
            out_specs=inside,
            scratch_shapes=[
                tile32,
                pltpu.VMEM((couples, width), jnp.int32),
                pltpu.VMEM((couples, width), jnp.int32),
                pltpu.VMEM((1, width), jnp.int32),
                pltpu.VMEM((1, width), jnp.int32),
                pltpu.VMEM((couples, unknowns, unknowns, width), jnp.bfloat16),
                pltpu.VMEM((couples, unknowns, unknowns, width), jnp.bfloat16),
                pltpu.VMEM((1, unknowns, unknowns, width), jnp.bfloat16),
                pltpu.VMEM((1, unknowns, unknowns, width), jnp.bfloat16),
                gathered,
                gathered,
                gathered,
                gathered,
                pltpu.VMEM((wide_count, 1, width), jnp.int32),
                tile16,
                tile16,
                tile16,
                pltpu.VMEM((couples, unknowns, width), jnp.float32),
                pltpu.VMEM((1, unknowns, width), jnp.float32),
                tile32,
                tile32,
                tile32,
                pltpu.VMEM((wide_count, width, width), jnp.bfloat16),
                pltpu.VMEM((wide_count, width, width), jnp.bfloat16),
                pltpu.VMEM((wide_count, width, couples * width), jnp.bfloat16),
                pltpu.VMEM((wide_count, width, couples * width), jnp.bfloat16),
                pltpu.SemaphoreType.DMA((9,)),
                pltpu.SemaphoreType.DMA((7, wide_count)),
                pltpu.SemaphoreType.DMA((7, wide_count)),
            ],
            compiler_params=pltpu.CompilerParams(
                collective_id=0, has_side_effects=True, vmem_limit_bytes=63 * 1024 * 1024
            ),
        )(rhs, lower, lower_index, upper, upper_index, inverse, donor, donor_index, target)

    return jax.shard_map(
        per_device, mesh=mesh, in_specs=in_specs, out_specs=out_specs, check_vma=False
    )
```
